32 devices in a mesh: prow: 4 (over y, x), pcol: 8 (over z, core).
Axes of the slice: x: 2, y: 2, z: 4, core: 2. Of those that a mesh axis runs over, the one named last changes fastest.
Arguments:
- latent: bfloat16 [16, 32, 1280], P('prow', 'pcol'), may hold values from -8 to 8
- norm_scale: float32 [3, 1280], replicated, may hold values from 0.25 to 1.75
- norm_shift: float32 [3, 1280], replicated, may hold values from -3 to 3
- time_shift: float32 [1280], replicated, may hold values from -4 to 4
- conv_bias: float32 [2, 1280], replicated, may hold values from -3 to 3
- conv_one: bfloat16 [3, 3, 1280, 1280], P(None, None, 'prow'), may hold values from -0.0546875 to 0.0546875
- conv_two: bfloat16 [3, 3, 1280, 1280], P(None, None, 'prow'), may hold values from -0.0546875 to 0.0546875
- w_qkv: bfloat16 [768, 1280], P('prow'), may hold values from -0.3125 to 0.3125
- w_out: bfloat16 [1280, 256], P('prow'), may hold values from -0.375 to 0.375
- stale_kv: bfloat16 [16, 32, 4, 128], P(None, 'pcol', 'prow'), may hold values from -36 to 36
Outputs:
- next_latent: bfloat16 [16, 32, 1280], P('prow', 'pcol')
- fresh_kv: bfloat16 [16, 32, 4, 128], P(None, 'pcol', 'prow')
The draws below stay inside these ranges and needn't reach their ends.
All inputs are finite; a program needn't handle non-finite values.
Results may differ from the reference program's by a relative error of at most 0.028.
Values may be sent and summed in bfloat16 or wider, within the bound.
A program may use at most 64 MiB of HBM per device.

```python
import jax
import jax.numpy as jnp
from jax import lax

C = 1280
GROUPS = 32
HEAD = 64
PC = 4
HEADS = 4
LH = 16
LW = 32
N_PCOL = 8


def draw_latent(key, part):
    first = jax.random.fold_in(jax.random.fold_in(key, 11), 0)
    rows = jnp.arange(LH, dtype=jnp.float32)[:, None] / LH
    cols = jnp.arange(LW, dtype=jnp.float32)[None, :] / LW
    ramp = (3.0 ** (0.5 * (rows + cols)))[:, :, None]
    value = jax.random.normal(first, (LH, LW, C), jnp.float32) * ramp * 0.6
    return jnp.clip(value, -8.0, 8.0).astype(jnp.bfloat16)


def draw_stale_kv(key, part):
    parts = jax.random.split(jax.random.fold_in(key, 23), 1)
    shape = (LH, LW, HEADS, 2 * HEAD)
    base = jax.random.normal(parts[0], shape, jnp.float32) * 1.7
    return jnp.clip(base, -36.0, 36.0).astype(jnp.bfloat16)


def level_of(key, shape, cuts, smallest, largest):
    level, own = 1.0, jax.random.fold_in(key, 6)
    for axis_at, blocks in cuts:
        steps = jnp.exp(jax.random.uniform(jax.random.fold_in(own, axis_at), (blocks,), jnp.float32, smallest / len(cuts), largest / len(cuts)))
        level = level * jnp.repeat(steps, shape[axis_at] // blocks).reshape([-1 if axis == axis_at else 1 for axis in range(len(shape))])
    return level


def scatter_about(stream_key, dims, spread, bound, cuts=(), kind=jnp.bfloat16):
    drawn = spread * jax.random.normal(stream_key, dims, jnp.float32)
    if cuts:
        drawn = drawn * level_of(stream_key, dims, cuts, -0.22, 0.18)
    return jnp.clip(drawn, -bound, bound).astype(kind)


def setup_inputs(seed: int = 0) -> dict:
    key_of = jax.random.split(jax.random.key(seed), 11)
    return {
        "latent": draw_latent(jax.random.fold_in(key_of[10], 71), 0),
        "norm_scale": jnp.clip(1.0 + 0.15 * jax.random.normal(key_of[1], (3, C), jnp.float32), 0.25, 1.75),
        "norm_shift": scatter_about(key_of[2], (3, C), 0.5, 3.0, (), jnp.float32),
        "time_shift": scatter_about(key_of[3], (C,), 1.0, 4.0, (), jnp.float32),
        "conv_bias": scatter_about(key_of[4], (2, C), 0.5, 3.0, (), jnp.float32),
        "conv_one": scatter_about(key_of[5], (3, 3, C, C), (9 * C) ** -0.5, 0.0546875, ((2, 4),)),
        "conv_two": scatter_about(key_of[6], (3, 3, C, C), (9 * C) ** -0.5, 0.0546875, ((2, 4),)),
        "w_qkv": scatter_about(key_of[7], (HEADS * 3 * HEAD, C), (C // 3) ** -0.5, 0.3125, ((0, 4),)),
        "w_out": scatter_about(key_of[8], (C, HEADS * HEAD), (HEADS * HEAD) ** -0.5, 0.375, ((0, 4),)),
        "stale_kv": draw_stale_kv(jax.random.fold_in(key_of[10], 71), 0),
    }


EPSILON = 1e-05

def group_norm(field, scale, shift):
    grouped = field.reshape(LH * LW, GROUPS, C // GROUPS)
    average = lax.optimization_barrier(jnp.mean(grouped, axis=(0, 2)))
    centered = grouped - average[None, :, None]
    variance = lax.optimization_barrier(jnp.mean(centered * centered, axis=(0, 2)))
    normed = centered * lax.rsqrt(variance + EPSILON)[None, :, None]
    return normed.reshape(LH, LW, C) * scale + shift

def convolve(field, weight):
    padded = jnp.pad(field, ((1, 1), (1, 1), (0, 0)))
    taps = [padded[row_tap:row_tap + LH, col_tap:col_tap + LW, :] for row_tap in range(3) for col_tap in range(3)]
    stacked = jnp.concatenate(taps, axis=-1).reshape(LH * LW, 9 * C)
    matrix = jnp.transpose(weight, (0, 1, 3, 2)).reshape(9 * C, C)
    result = jnp.dot(stacked, matrix, preferred_element_type=jnp.float32)
    return result.reshape(LH, LW, C)

def reference(latent, norm_scale, norm_shift, time_shift, conv_bias, conv_one, conv_two, w_qkv, w_out, stale_kv):
    inputs = latent.astype(jnp.float32)
    first_act = jax.nn.silu(group_norm(inputs, norm_scale[0], norm_shift[0])).astype(jnp.bfloat16)
    first_conv = convolve(first_act, conv_one) + conv_bias[0] + time_shift
    second_act = jax.nn.silu(group_norm(first_conv, norm_scale[1], norm_shift[1])).astype(jnp.bfloat16)
    resnet_out = (inputs + convolve(second_act, conv_two) + conv_bias[1]).astype(jnp.bfloat16)
    attn_in = group_norm(resnet_out.astype(jnp.float32), norm_scale[2], norm_shift[2]).astype(jnp.bfloat16)
    qkv = jnp.dot(attn_in.reshape(LH * LW, C), w_qkv.T, preferred_element_type=jnp.float32).astype(jnp.bfloat16)
    qkv = qkv.reshape(LH, LW, HEADS, 3, HEAD)
    queries = qkv[:, :, :, 0, :]
    fresh_kv = jnp.concatenate([qkv[:, :, :, 1, :], qkv[:, :, :, 2, :]], axis=-1)
    scale = HEAD ** (-0.5)

    def strip_attend(strip):
        start = (strip * PC).astype(jnp.int32)
        strip_queries = lax.dynamic_slice_in_dim(queries, start, PC, 1).reshape(LH * PC, HEADS, HEAD)
        fresh_strip = lax.dynamic_slice_in_dim(fresh_kv, start, PC, 1)
        pairs = lax.dynamic_update_slice_in_dim(stale_kv, fresh_strip, start, 1).reshape(LH * LW, HEADS, 2 * HEAD)
        keys = pairs[:, :, :HEAD].astype(jnp.float32)
        values = pairs[:, :, HEAD:].astype(jnp.float32)
        scores = jnp.einsum('qhd,khd->hqk', strip_queries.astype(jnp.float32), keys) * scale
        highest = lax.optimization_barrier(jnp.max(scores, axis=-1))
        weights = jnp.exp(scores - highest[..., None])
        denominator = lax.optimization_barrier(jnp.sum(weights, axis=-1))
        probs = weights.astype(jnp.bfloat16).astype(jnp.float32)
        weighted = jnp.einsum('hqk,khd->qhd', probs, values)
        return (weighted / denominator.T[..., None]).astype(jnp.bfloat16)
    attended = lax.map(strip_attend, jnp.arange(N_PCOL, dtype=jnp.int32))
    attended = attended.reshape(N_PCOL, LH, PC, HEADS * HEAD).transpose(1, 0, 2, 3).reshape(LH * LW, HEADS * HEAD)
    added = jnp.dot(attended, w_out.T, preferred_element_type=jnp.float32)
    next_latent = (resnet_out.astype(jnp.float32).reshape(LH * LW, C) + added).astype(jnp.bfloat16).reshape(LH, LW, C)
    return (next_latent, fresh_kv)
```

```python
import functools

import jax
import jax.numpy as jnp
from jax import lax
from jax.experimental import pallas as pl
from jax.experimental.pallas import tpu as pltpu
from jax.sharding import PartitionSpec as P

GROUPS = 32
HEAD = 64


EPSILON = 1e-05


def padded(cells, sides, width):
    for axis, dim in sides:
        count = lax.axis_size(axis)
        ends = count - 1
        head = lax.slice_in_dim(cells, 0, width, axis=dim)
        tail = lax.slice_in_dim(cells, cells.shape[dim] - width, cells.shape[dim], axis=dim)
        cells = jnp.concatenate(
            [
                lax.ppermute(tail, axis, [(i, (i + 1) % count) for i in range(ends)]),
                cells,
                lax.ppermute(head, axis, [((i + 1) % count, i) for i in range(ends)]),
            ],
            axis=dim,
        )
    return cells


def times_rows(left, right):
    return lax.dot_general(
        left, right, (((1,), (1,)), ((), ())), preferred_element_type=jnp.float32
    )


def group_norm(field, scale, shift, population):
    rows_here, cols_here, width = field.shape
    grouped = field.reshape(rows_here * cols_here, GROUPS, width // GROUPS)
    summed, squared = lax.psum(
        (jnp.sum(grouped, axis=(0, 2)), jnp.sum(grouped * grouped, axis=(0, 2))), ("prow", "pcol")
    )
    average = summed / population
    variance = squared / population - average * average
    centered = grouped - average[None, :, None]
    normed = centered * lax.rsqrt(variance + EPSILON)[None, :, None]
    return normed.reshape(field.shape) * scale + shift


def conv_terms(field, weight):
    rows_here, cols_here, width = field.shape
    out_width = weight.shape[2]
    parties = lax.axis_size("prow")
    cells = rows_here * cols_here
    framed_patch = padded(field, (("prow", 0), ("pcol", 1)), 1)
    stacked = lax.all_gather(framed_patch[None], "prow", axis=0, tiled=True)
    total = jnp.zeros((parties * cells, out_width), jnp.float32)
    for row_tap in range(3):
        for col_tap in range(3):
            total = total + times_rows(
                stacked[:, row_tap : row_tap + rows_here, col_tap : col_tap + cols_here, :].reshape(
                    -1, width
                ),
                weight[row_tap, col_tap],
            )
    returned = lax.all_to_all(
        total.reshape(parties, cells, out_width).astype(jnp.bfloat16),
        "prow",
        split_axis=0,
        concat_axis=2,
        tiled=True,
    ).astype(jnp.float32)
    return returned.reshape(cells, parties * out_width)


def partial_softmax(queries, pairs, scale):
    keys = pairs[..., :HEAD]
    values = pairs[..., HEAD:]
    scores = jnp.einsum("qhd,khd->hqk", queries, keys, preferred_element_type=jnp.float32) * scale
    highest = jnp.max(scores, axis=-1)
    weights = jnp.exp(scores - highest[..., None])
    denominator = jnp.sum(weights, axis=-1)
    weighted = jnp.einsum(
        "hqk,khd->qhd", weights.astype(jnp.bfloat16), values, preferred_element_type=jnp.float32
    )
    return (highest, denominator, weighted)


def shards(
    latent,
    norm_scale,
    norm_shift,
    time_shift,
    conv_bias,
    conv_one,
    conv_two,
    w_qkv,
    w_out,
    stale_kv,
):
    rows_here, cols_here, width = latent.shape
    cells = rows_here * cols_here
    parties = lax.axis_size("prow")
    population = float(cells * lax.axis_size("prow") * lax.axis_size("pcol") * (width // GROUPS))
    inputs = latent.astype(jnp.float32)
    first_act = jax.nn.silu(group_norm(inputs, norm_scale[0], norm_shift[0], population)).astype(
        jnp.bfloat16
    )
    first_conv = conv_terms(first_act, conv_one).reshape(latent.shape) + conv_bias[0] + time_shift
    second_act = jax.nn.silu(
        group_norm(first_conv, norm_scale[1], norm_shift[1], population)
    ).astype(jnp.bfloat16)
    second_conv = conv_terms(second_act, conv_two).reshape(latent.shape) + conv_bias[1]
    resnet_out = (inputs + second_conv).astype(jnp.bfloat16)
    attn_in = group_norm(
        resnet_out.astype(jnp.float32), norm_scale[2], norm_shift[2], population
    ).astype(jnp.bfloat16)
    column_width = w_qkv.shape[0]
    heads_here = column_width // (3 * HEAD)
    piece = lax.all_gather(attn_in, "prow", axis=0, tiled=True)
    mapped = times_rows(piece.reshape(-1, width), w_qkv)
    strip_qkv = mapped.astype(jnp.bfloat16).reshape(piece.shape[0], cols_here, column_width)
    strip_rows = strip_qkv.shape[0]
    parted = strip_qkv.reshape(strip_rows * cols_here, heads_here, 3, HEAD)
    queries = parted[:, :, 0, :]
    fresh = jnp.concatenate([parted[:, :, 1, :], parted[:, :, 2, :]], axis=-1)
    scale = HEAD ** (-0.5)
    column = lax.axis_index("pcol")
    initial = partial_softmax(queries, fresh, scale)
    piece = lax.all_gather(stale_kv, "pcol", axis=1, tiled=True)
    highest, denominator, weighted = initial
    columns = lax.iota(jnp.int32, piece.shape[1])
    foreign = jnp.broadcast_to((columns // cols_here != column)[None, :], piece.shape[:2]).reshape(
        -1
    )
    pairs = piece.reshape(-1, heads_here, 2 * HEAD)
    scores = (
        jnp.einsum("qhd,khd->hqk", queries, pairs[:, :, :HEAD], preferred_element_type=jnp.float32)
        * scale
    )
    scores = jnp.where(foreign[None, None, :], scores, -jnp.inf)
    raised = jnp.maximum(highest, jnp.max(scores, axis=-1))
    factor = jnp.exp(highest - raised)
    weights = jnp.exp(scores - raised[..., None])
    denominator = denominator * factor + jnp.sum(weights, axis=-1)
    update = jnp.einsum(
        "hqk,khd->qhd",
        weights.astype(jnp.bfloat16),
        pairs[:, :, HEAD:],
        preferred_element_type=jnp.float32,
    )
    weighted = weighted * factor.T[..., None] + update
    highest, denominator, weighted = (raised, denominator, weighted)
    attended = (
        (weighted / denominator.T[..., None]).astype(jnp.bfloat16).reshape(-1, heads_here * HEAD)
    )
    out_width = w_out.shape[0]
    summed = times_rows(lax.all_gather(attended, "prow", axis=1, tiled=True), w_out)
    added = (
        lax.all_to_all(
            summed.reshape(parties, cells, out_width).astype(jnp.bfloat16),
            "prow",
            split_axis=0,
            concat_axis=2,
            tiled=True,
        )
        .astype(jnp.float32)
        .reshape(cells, width)
    )
    next_latent = (
        (resnet_out.astype(jnp.float32).reshape(cells, width) + added)
        .astype(jnp.bfloat16)
        .reshape(latent.shape)
    )
    return (next_latent, fresh.reshape(strip_rows, cols_here, heads_here, 2 * HEAD))


LANES = 256
MESH = pl.DeviceIdType.MESH
BF = jnp.bfloat16
F32 = jnp.float32


def fits(mesh, latent, *rest):
    rows, cols, width = latent.shape
    conv_one, w_qkv, w_out = rest[4], rest[6], rest[7]
    rows_all = rows * mesh.shape["prow"]
    block = conv_one.shape[2]
    return (
        mesh.size <= 64
        and rows_all % 16 == 0
        and (rows * cols) % 16 == 0
        and width % LANES == 0
        and block % (width // GROUPS) == 0
        and w_qkv.shape[0] == 3 * HEAD
        and w_out.shape[0] == block
        and 4 * conv_one.size < 32 * 2**20
    )


def matmul(left, right):
    return lax.dot_general(left, right, (((1,), (0,)), ((), ())), preferred_element_type=F32)


def iota2(shape, dim):
    return lax.broadcasted_iota(jnp.int32, shape, dim)


def one_hot(mask):
    return jnp.where(mask, 1.0, 0.0).astype(BF)


def split_terms(value):
    high = value.astype(BF)
    rest = value - high.astype(F32)
    middle = rest.astype(BF)
    low = (rest - middle.astype(F32)).astype(BF)
    return high, middle, low


def remote(src, dst, send, recv, row, col):
    return pltpu.make_async_remote_copy(
        src_ref=src,
        dst_ref=dst,
        send_sem=send,
        recv_sem=recv,
        device_id=(row, col),
        device_id_type=MESH,
    )


def fused_kernel(
    dims,
    lat_ref,
    scale_ref,
    shift_ref,
    time_ref,
    bias_ref,
    one_ref,
    two_ref,
    qkv_ref,
    out_w_ref,
    stale_ref,
    next_ref,
    fresh_ref,
    w_one,
    w_two,
    w_in,
    w_back,
    patches,
    edge_out,
    edges,
    strip,
    acts,
    raw,
    res,
    pairs,
    att_out,
    att,
    stats,
    groups_of,
    w_sem,
    stat_send,
    stat_recv,
    row_send,
    row_recv,
    edge_send,
    edge_recv,
    pair_send,
    pair_recv,
):
    parties, strips, rows, cols, width, block = dims
    total = parties * strips
    rows_all = parties * rows
    cells = rows * cols
    strip_cells = rows_all * cols
    halo_cells = rows_all * (cols + 2)
    size = width // GROUPS
    count = float(strip_cells * strips * size)
    row_me, col_me = lax.axis_index("prow"), lax.axis_index("pcol")
    me = row_me * strips + col_me
    pad = edge_out.shape[1]
    parts = width // LANES

    def peer(k):
        other = lax.rem(me + k, total)
        return lax.div(other, strips), lax.rem(other, strips)

    barrier = pltpu.get_barrier_semaphore()
    for k in range(1, total):
        pl.semaphore_signal(barrier, inc=1, device_id=peer(k), device_id_type=MESH)

    taps = [(a, b) for a in range(3) for b in range(3)]
    loads = [
        [
            pltpu.make_async_copy(ref.at[a, b], buf.at[3 * a + b], w_sem.at[9 * which + 3 * a + b])
            for a, b in taps
        ]
        for which, (ref, buf) in enumerate(((one_ref, w_one), (two_ref, w_two)))
    ]
    for load in loads[0]:
        load.start()
    load_in = pltpu.make_async_copy(qkv_ref, w_in, w_sem.at[18])
    load_back = pltpu.make_async_copy(out_w_ref, w_back.at[row_me], w_sem.at[19])
    load_back.start()
    for load in loads[1]:
        load.start()
    load_in.start()

    channel = iota2((width, 128), 0)
    group = iota2((width, 128), 1) * size
    groups_of[...] = one_hot((channel >= group) & (channel < group + size))
    channel = iota2((block, 128), 0) + row_me * block
    group = iota2((block, 128), 1) * size
    block_groups = one_hot((channel >= group) & (channel < group + size))

    def send_stats(which, field, members):
        sums = jnp.concatenate(
            [
                jnp.sum(field, axis=0, keepdims=True),
                jnp.sum(field * field, axis=0, keepdims=True),
                jnp.zeros((6, field.shape[1]), F32),
            ],
            axis=0,
        )
        gathered = sum(matmul(term, members) for term in split_terms(sums))
        stats[which, 0] = gathered[:2]

    def stat_copies(which):
        return [
            remote(
                stats.at[which, 0],
                stats.at[which, k],
                stat_send.at[which, k],
                stat_recv.at[which, k],
                *peer(k),
            )
            for k in range(1, total)
        ]

    def norm(which, field):
        both = jnp.sum(stats[which], axis=0) / count
        average = both[0:1]
        inverse = lax.rsqrt(both[1:2] - average * average + EPSILON)
        line = jnp.concatenate([average, inverse, jnp.zeros((6, 128), F32)], axis=0)
        wide = sum(times_rows(term, groups_of[...]) for term in split_terms(line))
        gain = wide[1:2] * scale_ref[which : which + 1]
        return (field - wide[0:1]) * gain + shift_ref[which : which + 1]

    def mine(field):
        picked = field[:, :block]
        for other in range(1, parties):
            part = field[:, other * block : (other + 1) * block]
            picked = jnp.where(row_me == other, part, picked)
        return picked

    own = jnp.concatenate([lat_ref[i].astype(F32) for i in range(rows)], axis=0)
    own_b = own.astype(BF)
    patches[row_me] = own_b
    send_stats(0, own, groups_of[...])
    packed = jnp.zeros((2 * pad, LANES), F32)
    for j in range(parts):
        at, source = iota2((2 * pad, cells), 0), iota2((2 * pad, cells), 1)
        side = jnp.where(at >= pad, 1, 0)
        row = at - side * pad - j * rows
        wanted = row * cols + side * (cols - 1)
        chosen = one_hot((source == wanted) & (row >= 0) & (row < rows))
        packed = packed + matmul(chosen, own_b[:, j * LANES : (j + 1) * LANES])
    edge_out[0] = packed[:pad].astype(BF)
    edge_out[1] = packed[pad:].astype(BF)

    @pl.when(col_me == 0)
    def _():
        edges[0] = jnp.zeros(edges.shape[1:], BF)

    @pl.when(col_me == strips - 1)
    def _():
        edges[1] = jnp.zeros(edges.shape[1:], BF)

    pl.semaphore_wait(barrier, total - 1)

    def along(k):
        return lax.rem(row_me + k, parties)

    def row_copies(which, pick_src, pick_dst):
        return [
            remote(
                pick_src(along(k)),
                pick_dst(row_me),
                row_send.at[which, k],
                row_recv.at[which, k],
                along(k),
                col_me,
            )
            for k in range(1, parties)
        ]

    def edge_copies(which, src, dst):
        return [
            [
                remote(
                    src(side),
                    dst(1 - side),
                    edge_send.at[which, side, k],
                    edge_recv.at[which, side, k],
                    along(k),
                    jnp.maximum(col_me - 1, 0)
                    if side == 0
                    else jnp.minimum(col_me + 1, strips - 1),
                )
                for k in range(parties)
            ]
            for side in range(2)
        ]

    def run_edges(copies, action):
        for side in range(2):
            sends = (col_me > 0) if side == 0 else (col_me < strips - 1)
            takes = (col_me < strips - 1) if side == 0 else (col_me > 0)

            @pl.when(takes if action == "recv" else sends)
            def _():
                for copy in copies[side]:
                    if action == "start":
                        copy.start()
                    elif action == "recv":
                        copy.wait_recv()
                    else:
                        copy.wait_send()

    stat0 = stat_copies(0)
    patch0 = row_copies(0, lambda t: patches.at[row_me], lambda me_row: patches.at[me_row])
    edge0 = edge_copies(0, lambda s: edge_out.at[s], lambda s: edges.at[s, row_me])
    for copy in stat0:
        copy.start()
    for copy in patch0:
        copy.start()
    run_edges(edge0, "start")

    for copy in patch0:
        copy.wait_recv()
    run_edges(edge0, "recv")

    at, source = iota2((strip_cells, strip_cells), 0), iota2((strip_cells, strip_cells), 1)
    at_col, at_row = lax.div(at, rows_all), lax.rem(at, rows_all)
    to_columns = one_hot(source == at_row * cols + at_col)
    at_row, at_col = lax.div(at, cols), lax.rem(at, cols)
    to_rows = one_hot(source == at_col * rows_all + at_row)

    strip[rows_all : rows_all + strip_cells] = matmul(
        to_columns, patches[...].reshape(strip_cells, width)
    )
    arrived = edges[...].reshape(2 * parties * pad, LANES)
    at = iota2((2 * rows_all, 2 * parties * pad), 0)
    source = iota2((2 * rows_all, 2 * parties * pad), 1)
    for j in range(parts):
        chosen = one_hot(source == lax.div(at, rows) * pad + j * rows + lax.rem(at, rows))
        part = matmul(chosen, arrived)
        span = slice(j * LANES, (j + 1) * LANES)
        strip[:rows_all, span] = part[:rows_all]
        strip[rows_all + strip_cells :, span] = part[rows_all:]

    for copy in stat0:
        copy.wait_recv()

    where_at = iota2((halo_cells, 1), 0)
    outside = ((where_at < rows_all) & (col_me == 0)) | (
        (where_at >= rows_all + strip_cells) & (col_me == strips - 1)
    )
    in_column = lax.rem(where_at, rows_all)

    def activate(which, field):
        normed = norm(which, field)
        act = jnp.where(outside, 0.0, normed / (1.0 + jnp.exp(-normed)))
        acts[1] = act.astype(BF)
        acts[0] = jnp.where(in_column == 0, 0.0, pltpu.roll(act, 1, 0)).astype(BF)
        acts[2] = jnp.where(
            in_column == rows_all - 1, 0.0, pltpu.roll(act, halo_cells - 1, 0)
        ).astype(BF)

    def convolve(which, weights):
        result = jnp.zeros((strip_cells, block), F32)
        for a, b in taps:
            loads[which][3 * a + b].wait()
            result = result + times_rows(
                acts[a, b * rows_all : b * rows_all + strip_cells], weights[3 * a + b]
            )
        return result

    activate(0, strip[...])

    load_back.wait()
    back = row_copies(3, lambda t: w_back.at[row_me], lambda me_row: w_back.at[me_row])
    pair_copies = [
        remote(
            stale_ref,
            pairs.at[col_me],
            pair_send.at[k],
            pair_recv.at[k],
            row_me,
            lax.rem(col_me + k, strips),
        )
        for k in range(1, strips)
    ]
    for copy in pair_copies:
        copy.start()
    for copy in back:
        copy.start()

    first = convolve(0, w_one)
    offset = bias_ref[0:1] + time_ref[...]
    middle = pl.ds(rows_all, strip_cells)
    raw[row_me, rows_all : rows_all + strip_cells] = first.astype(BF)
    raw1 = row_copies(1, lambda t: raw.at[row_me, middle], lambda me_row: raw.at[me_row, middle])
    ends_src = (pl.ds(rows_all, rows_all), pl.ds(strip_cells, rows_all))
    ends_dst = (pl.ds(0, rows_all), pl.ds(rows_all + strip_cells, rows_all))
    edge1 = edge_copies(
        1, lambda s: raw.at[row_me, ends_src[s]], lambda s: raw.at[row_me, ends_dst[s]]
    )
    for copy in raw1:
        copy.start()
    run_edges(edge1, "start")
    send_stats(1, first + mine(offset), block_groups)
    stat1 = stat_copies(1)
    for copy in stat1:
        copy.start()

    @pl.when(col_me == 0)
    def _():
        raw[:, :rows_all] = jnp.zeros((parties, rows_all, block), BF)

    @pl.when(col_me == strips - 1)
    def _():
        raw[:, rows_all + strip_cells :] = jnp.zeros((parties, rows_all, block), BF)

    residual = mine(strip[rows_all : rows_all + strip_cells]) + mine(bias_ref[1:2])

    for copy in raw1:
        copy.wait_recv()
    run_edges(edge1, "recv")
    field = jnp.concatenate([raw[i].astype(F32) for i in range(parties)], axis=1) + offset
    for copy in stat1:
        copy.wait_recv()
    activate(1, field)
    second = convolve(1, w_two)

    rounded = (residual + second).astype(BF)
    res[row_me] = rounded
    res2 = row_copies(2, lambda t: res.at[row_me], lambda me_row: res.at[me_row])
    for copy in res2:
        copy.start()
    send_stats(2, rounded.astype(F32), block_groups)
    stat2 = stat_copies(2)
    for copy in stat2:
        copy.start()
    for copy in res2:
        copy.wait_recv()
    field = jnp.concatenate([res[i].astype(F32) for i in range(parties)], axis=1)
    at, source = iota2((cells, strip_cells), 0), iota2((cells, strip_cells), 1)
    patch_row = row_me * rows + lax.div(at, cols)
    chosen = one_hot(source == lax.rem(at, cols) * rows_all + patch_row)
    kept = matmul(chosen, field.astype(BF))
    load_in.wait()
    for copy in stat2:
        copy.wait_recv()
    attn_in = norm(2, field).astype(BF)

    queries = times_rows(attn_in, w_in[:HEAD]).astype(BF)
    fresh = times_rows(attn_in, w_in[HEAD:]).astype(BF)
    for copy in pair_copies:
        copy.wait_recv()
    pairs[col_me] = fresh
    fresh_ref[...] = matmul(to_rows, fresh).astype(BF)
    both = pairs[...].reshape(strips * strip_cells, 2 * HEAD)
    scores = times_rows(queries, both[:, :HEAD]) * (HEAD**-0.5)
    weights = jnp.exp(scores - jnp.max(scores, axis=1, keepdims=True))
    denominator = jnp.sum(weights, axis=1, keepdims=True)
    attended = (matmul(weights.astype(BF), both) / denominator)[:, HEAD:].astype(BF)
    att_out[...] = (
        matmul(to_rows, attended).astype(BF).reshape(parties, cells, HEAD)
    )
    att3 = row_copies(4, lambda t: att_out.at[t], lambda me_row: att.at[me_row])
    for copy in att3:
        copy.start()
    att[row_me] = att_out[row_me]
    for copy in back:
        copy.wait_recv()
    for copy in att3:
        copy.wait_recv()
    heads = jnp.concatenate([att[i].astype(F32) for i in range(parties)], axis=1).astype(BF)
    added = jnp.concatenate([times_rows(heads, w_back[i]) for i in range(parties)], axis=1)
    result = kept + added
    for i in range(rows):
        next_ref[i] = result[i * cols : (i + 1) * cols].astype(BF)

    for copy in stat0 + stat1 + stat2 + patch0 + raw1 + res2 + back + att3 + pair_copies:
        copy.wait_send()
    run_edges(edge0, "send")
    run_edges(edge1, "send")


def fused(
    latent,
    norm_scale,
    norm_shift,
    time_shift,
    conv_bias,
    conv_one,
    conv_two,
    w_qkv,
    w_out,
    stale_kv,
):
    rows, cols, width = latent.shape
    block = conv_one.shape[2]
    parties, strips = lax.axis_size("prow"), lax.axis_size("pcol")
    total = parties * strips
    rows_all = rows * parties
    cells = rows * cols
    strip_cells = rows_all * cols
    halo_cells = rows_all * (cols + 2)
    pad = -(-rows * (width // LANES) // 16) * 16
    dims = (parties, strips, rows, cols, width, block)
    vmem = pl.BlockSpec(memory_space=pltpu.VMEM)
    anywhere = pl.BlockSpec(memory_space=pl.ANY)
    dma = pltpu.SemaphoreType.DMA
    next_latent, fresh = pl.pallas_call(
        functools.partial(fused_kernel, dims),
        out_shape=(
            jax.ShapeDtypeStruct(latent.shape, BF),
            jax.ShapeDtypeStruct((strip_cells, 2 * HEAD), BF),
        ),
        in_specs=[vmem] * 5 + [anywhere] * 4 + [vmem],
        out_specs=(vmem, vmem),
        scratch_shapes=[
            pltpu.VMEM((9, block, width), BF),
            pltpu.VMEM((9, block, width), BF),
            pltpu.VMEM(w_qkv.shape, BF),
            pltpu.VMEM((parties,) + w_out.shape, BF),
            pltpu.VMEM((parties, cells, width), BF),
            pltpu.VMEM((2, pad, LANES), BF),
            pltpu.VMEM((2, parties, pad, LANES), BF),
            pltpu.VMEM((halo_cells, width), F32),
            pltpu.VMEM((3, halo_cells, width), BF),
            pltpu.VMEM((parties, halo_cells, block), BF),
            pltpu.VMEM((parties, strip_cells, block), BF),
            pltpu.VMEM((strips, strip_cells, 2 * HEAD), BF),
            pltpu.VMEM((parties, cells, HEAD), BF),
            pltpu.VMEM((parties, cells, HEAD), BF),
            pltpu.VMEM((3, total, 2, 128), F32),
            pltpu.VMEM((width, 128), BF),
            dma((20,)),
            dma((3, total)),
            dma((3, total)),
            dma((5, parties)),
            dma((5, parties)),
            dma((2, 2, parties)),
            dma((2, 2, parties)),
            dma((strips,)),
            dma((strips,)),
        ],
        compiler_params=pltpu.CompilerParams(
            collective_id=0, has_side_effects=True, vmem_limit_bytes=48 * 2**20
        ),
    )(
        latent,
        norm_scale,
        norm_shift,
        time_shift.reshape(1, width),
        conv_bias,
        conv_one,
        conv_two,
        w_qkv,
        w_out,
        stale_kv.reshape(strip_cells, 2 * HEAD),
    )
    return next_latent, fresh.reshape(rows_all, cols, 1, 2 * HEAD)


def solution(mesh):
    placed = (
        P("prow", "pcol", None),
        P(),
        P(),
        P(),
        P(),
        P(None, None, "prow", None),
        P(None, None, "prow", None),
        P("prow", None),
        P("prow", None),
        P(None, "pcol", "prow", None),
    )

    def body(*args):
        return (fused if fits(mesh, *args) else shards)(*args)

    return jax.shard_map(
        body,
        mesh=mesh,
        in_specs=placed,
        out_specs=(P("prow", "pcol", None), P(None, "pcol", "prow", None)),
        check_vma=False,
    )
```

```python
import functools

import jax
import jax.numpy as jnp
from jax import lax
from jax.experimental import pallas as pl
from jax.experimental.pallas import tpu as pltpu
from jax.sharding import PartitionSpec as P

GROUPS = 32
HEAD = 64


EPSILON = 1e-05


def padded(cells, sides, width):
    for axis, dim in sides:
        count = lax.axis_size(axis)
        ends = count - 1
        head = lax.slice_in_dim(cells, 0, width, axis=dim)
        tail = lax.slice_in_dim(cells, cells.shape[dim] - width, cells.shape[dim], axis=dim)
        cells = jnp.concatenate(
            [
                lax.ppermute(tail, axis, [(i, (i + 1) % count) for i in range(ends)]),
                cells,
                lax.ppermute(head, axis, [((i + 1) % count, i) for i in range(ends)]),
            ],
            axis=dim,
        )
    return cells


def times_rows(left, right):
    return lax.dot_general(
        left, right, (((1,), (1,)), ((), ())), preferred_element_type=jnp.float32
    )


def group_norm(field, scale, shift, population):
    rows_here, cols_here, width = field.shape
    grouped = field.reshape(rows_here * cols_here, GROUPS, width // GROUPS)
    summed, squared = lax.psum(
        (jnp.sum(grouped, axis=(0, 2)), jnp.sum(grouped * grouped, axis=(0, 2))), ("prow", "pcol")
    )
    average = summed / population
    variance = squared / population - average * average
    centered = grouped - average[None, :, None]
    normed = centered * lax.rsqrt(variance + EPSILON)[None, :, None]
    return normed.reshape(field.shape) * scale + shift


def conv_terms(field, weight):
    rows_here, cols_here, width = field.shape
    out_width = weight.shape[2]
    parties = lax.axis_size("prow")
    cells = rows_here * cols_here
    framed_patch = padded(field, (("prow", 0), ("pcol", 1)), 1)
    stacked = lax.all_gather(framed_patch[None], "prow", axis=0, tiled=True)
    total = jnp.zeros((parties * cells, out_width), jnp.float32)
    for row_tap in range(3):
        for col_tap in range(3):
            total = total + times_rows(
                stacked[:, row_tap : row_tap + rows_here, col_tap : col_tap + cols_here, :].reshape(
                    -1, width
                ),
                weight[row_tap, col_tap],
            )
    returned = lax.all_to_all(
        total.reshape(parties, cells, out_width).astype(jnp.bfloat16),
        "prow",
        split_axis=0,
        concat_axis=2,
        tiled=True,
    ).astype(jnp.float32)
    return returned.reshape(cells, parties * out_width)


def partial_softmax(queries, pairs, scale):
    keys = pairs[..., :HEAD]
    values = pairs[..., HEAD:]
    scores = jnp.einsum("qhd,khd->hqk", queries, keys, preferred_element_type=jnp.float32) * scale
    highest = jnp.max(scores, axis=-1)
    weights = jnp.exp(scores - highest[..., None])
    denominator = jnp.sum(weights, axis=-1)
    weighted = jnp.einsum(
        "hqk,khd->qhd", weights.astype(jnp.bfloat16), values, preferred_element_type=jnp.float32
    )
    return (highest, denominator, weighted)


def shards(
    latent,
    norm_scale,
    norm_shift,
    time_shift,
    conv_bias,
    conv_one,
    conv_two,
    w_qkv,
    w_out,
    stale_kv,
):
    rows_here, cols_here, width = latent.shape
    cells = rows_here * cols_here
    parties = lax.axis_size("prow")
    population = float(cells * lax.axis_size("prow") * lax.axis_size("pcol") * (width // GROUPS))
    inputs = latent.astype(jnp.float32)
    first_act = jax.nn.silu(group_norm(inputs, norm_scale[0], norm_shift[0], population)).astype(
        jnp.bfloat16
    )
    first_conv = conv_terms(first_act, conv_one).reshape(latent.shape) + conv_bias[0] + time_shift
    second_act = jax.nn.silu(
        group_norm(first_conv, norm_scale[1], norm_shift[1], population)
    ).astype(jnp.bfloat16)
    second_conv = conv_terms(second_act, conv_two).reshape(latent.shape) + conv_bias[1]
    resnet_out = (inputs + second_conv).astype(jnp.bfloat16)
    attn_in = group_norm(
        resnet_out.astype(jnp.float32), norm_scale[2], norm_shift[2], population
    ).astype(jnp.bfloat16)
    column_width = w_qkv.shape[0]
    heads_here = column_width // (3 * HEAD)
    piece = lax.all_gather(attn_in, "prow", axis=0, tiled=True)
    mapped = times_rows(piece.reshape(-1, width), w_qkv)
    strip_qkv = mapped.astype(jnp.bfloat16).reshape(piece.shape[0], cols_here, column_width)
    strip_rows = strip_qkv.shape[0]
    parted = strip_qkv.reshape(strip_rows * cols_here, heads_here, 3, HEAD)
    queries = parted[:, :, 0, :]
    fresh = jnp.concatenate([parted[:, :, 1, :], parted[:, :, 2, :]], axis=-1)
    scale = HEAD ** (-0.5)
    column = lax.axis_index("pcol")
    initial = partial_softmax(queries, fresh, scale)
    piece = lax.all_gather(stale_kv, "pcol", axis=1, tiled=True)
    highest, denominator, weighted = initial
    columns = lax.iota(jnp.int32, piece.shape[1])
    foreign = jnp.broadcast_to((columns // cols_here != column)[None, :], piece.shape[:2]).reshape(
        -1
    )
    pairs = piece.reshape(-1, heads_here, 2 * HEAD)
    scores = (
        jnp.einsum("qhd,khd->hqk", queries, pairs[:, :, :HEAD], preferred_element_type=jnp.float32)
        * scale
    )
    scores = jnp.where(foreign[None, None, :], scores, -jnp.inf)
    raised = jnp.maximum(highest, jnp.max(scores, axis=-1))
    factor = jnp.exp(highest - raised)
    weights = jnp.exp(scores - raised[..., None])
    denominator = denominator * factor + jnp.sum(weights, axis=-1)
    update = jnp.einsum(
        "hqk,khd->qhd",
        weights.astype(jnp.bfloat16),
        pairs[:, :, HEAD:],
        preferred_element_type=jnp.float32,
    )
    weighted = weighted * factor.T[..., None] + update
    highest, denominator, weighted = (raised, denominator, weighted)
    attended = (
        (weighted / denominator.T[..., None]).astype(jnp.bfloat16).reshape(-1, heads_here * HEAD)
    )
    out_width = w_out.shape[0]
    summed = times_rows(lax.all_gather(attended, "prow", axis=1, tiled=True), w_out)
    added = (
        lax.all_to_all(
            summed.reshape(parties, cells, out_width).astype(jnp.bfloat16),
            "prow",
            split_axis=0,
            concat_axis=2,
            tiled=True,
        )
        .astype(jnp.float32)
        .reshape(cells, width)
    )
    next_latent = (
        (resnet_out.astype(jnp.float32).reshape(cells, width) + added)
        .astype(jnp.bfloat16)
        .reshape(latent.shape)
    )
    return (next_latent, fresh.reshape(strip_rows, cols_here, heads_here, 2 * HEAD))


LANES = 256
MESH = pl.DeviceIdType.MESH
BF = jnp.bfloat16
F32 = jnp.float32


def fits(mesh, latent, *rest):
    rows, cols, width = latent.shape
    conv_one, w_qkv, w_out = rest[4], rest[6], rest[7]
    rows_all = rows * mesh.shape["prow"]
    block = conv_one.shape[2]
    return (
        mesh.size <= 64
        and rows_all % 16 == 0
        and (rows * cols) % 16 == 0
        and width % LANES == 0
        and block % (width // GROUPS) == 0
        and block % 32 == 0
        and w_qkv.shape[0] == 3 * HEAD
        and w_out.shape[0] == block
        and 4 * conv_one.size < 32 * 2**20
    )


def matmul(left, right):
    return lax.dot_general(left, right, (((1,), (0,)), ((), ())), preferred_element_type=F32)


def iota2(shape, dim):
    return lax.broadcasted_iota(jnp.int32, shape, dim)


def one_hot(mask):
    return jnp.where(mask, 1.0, 0.0).astype(BF)


def split_terms(value):
    high = value.astype(BF)
    rest = value - high.astype(F32)
    middle = rest.astype(BF)
    low = (rest - middle.astype(F32)).astype(BF)
    return high, middle, low


def remote(src, dst, send, recv, row, col):
    return pltpu.make_async_remote_copy(
        src_ref=src,
        dst_ref=dst,
        send_sem=send,
        recv_sem=recv,
        device_id=(row, col),
        device_id_type=MESH,
    )


def fused_kernel(
    dims,
    lat_in,
    scale_in,
    shift_in,
    time_in,
    bias_in,
    one_ref,
    two_ref,
    qkv_ref,
    out_w_ref,
    stale_ref,
    next_ref,
    fresh_ref,
    lat_ref,
    scale_ref,
    shift_ref,
    time_ref,
    bias_ref,
    w_one,
    w_two,
    w_in,
    w_back,
    patches,
    edge_out,
    edges,
    strip,
    acts,
    raw,
    res,
    pairs,
    att_out,
    att,
    stats,
    groups_of,
    w_sem,
    stat_send,
    stat_recv,
    row_send,
    row_recv,
    edge_send,
    edge_recv,
    pair_send,
    pair_recv,
):
    parties, strips, rows, cols, width, block = dims
    total = parties * strips
    rows_all = parties * rows
    cells = rows * cols
    strip_cells = rows_all * cols
    halo_cells = rows_all * (cols + 2)
    size = width // GROUPS
    count = float(strip_cells * strips * size)
    row_me, col_me = lax.axis_index("prow"), lax.axis_index("pcol")
    me = row_me * strips + col_me
    pad = edge_out.shape[1]
    parts = width // LANES

    def peer(k):
        other = lax.rem(me + k, total)
        return lax.div(other, strips), lax.rem(other, strips)

    small = [
        pltpu.make_async_copy(src, dst, w_sem.at[20 + i])
        for i, (src, dst) in enumerate(
            (
                (lat_in, lat_ref),
                (scale_in, scale_ref),
                (shift_in, shift_ref),
                (time_in, time_ref),
                (bias_in, bias_ref),
            )
        )
    ]
    for load in small:
        load.start()
    barrier = pltpu.get_barrier_semaphore()
    for k in range(1, total):
        pl.semaphore_signal(barrier, inc=1, device_id=peer(k), device_id_type=MESH)

    taps = [(a, b) for a in range(3) for b in range(3)]
    loads = [
        [
            pltpu.make_async_copy(ref.at[a, b], buf.at[3 * a + b], w_sem.at[9 * which + 3 * a + b])
            for a, b in taps
        ]
        for which, (ref, buf) in enumerate(((one_ref, w_one), (two_ref, w_two)))
    ]
    for load in loads[0]:
        load.start()
    load_in = pltpu.make_async_copy(qkv_ref, w_in, w_sem.at[18])
    load_back = pltpu.make_async_copy(out_w_ref, w_back.at[row_me], w_sem.at[19])
    load_back.start()
    for load in loads[1]:
        load.start()
    load_in.start()

    channel = iota2((width, 128), 0)
    group = iota2((width, 128), 1) * size
    groups_of[...] = one_hot((channel >= group) & (channel < group + size))
    channel = iota2((block, 128), 0) + row_me * block
    group = iota2((block, 128), 1) * size
    block_groups = one_hot((channel >= group) & (channel < group + size))

    def send_stats(which, field, members):
        sums = jnp.concatenate(
            [
                jnp.sum(field, axis=0, keepdims=True),
                jnp.sum(field * field, axis=0, keepdims=True),
                jnp.zeros((6, field.shape[1]), F32),
            ],
            axis=0,
        )
        gathered = sum(matmul(term, members) for term in split_terms(sums))
        stats[which, 0] = gathered[:2]

    def stat_copies(which):
        return [
            remote(
                stats.at[which, 0],
                stats.at[which, k],
                stat_send.at[which, k],
                stat_recv.at[which, k],
                *peer(k),
            )
            for k in range(1, total)
        ]

    def norm(which, field):
        both = jnp.sum(stats[which], axis=0) / count
        average = both[0:1]
        inverse = lax.rsqrt(both[1:2] - average * average + EPSILON)
        line = jnp.concatenate([average, inverse, jnp.zeros((6, 128), F32)], axis=0)
        wide = sum(times_rows(term, groups_of[...]) for term in split_terms(line))
        gain = wide[1:2] * scale_ref[which : which + 1]
        return (field - wide[0:1]) * gain + shift_ref[which : which + 1]

    def mine(field):
        picked = field[:, :block]
        for other in range(1, parties):
            part = field[:, other * block : (other + 1) * block]
            picked = jnp.where(row_me == other, part, picked)
        return picked

    for load in small:
        load.wait()
    own = jnp.concatenate([lat_ref[i].astype(F32) for i in range(rows)], axis=0)
    own_b = own.astype(BF)
    patches[row_me] = own_b
    send_stats(0, own, groups_of[...])
    packed = jnp.zeros((2 * pad, LANES), F32)
    for j in range(parts):
        at, source = iota2((2 * pad, cells), 0), iota2((2 * pad, cells), 1)
        side = jnp.where(at >= pad, 1, 0)
        row = at - side * pad - j * rows
        wanted = row * cols + side * (cols - 1)
        chosen = one_hot((source == wanted) & (row >= 0) & (row < rows))
        packed = packed + matmul(chosen, own_b[:, j * LANES : (j + 1) * LANES])
    edge_out[0] = packed[:pad].astype(BF)
    edge_out[1] = packed[pad:].astype(BF)

    @pl.when(col_me == 0)
    def _():
        edges[0] = jnp.zeros(edges.shape[1:], BF)

    @pl.when(col_me == strips - 1)
    def _():
        edges[1] = jnp.zeros(edges.shape[1:], BF)

    pl.semaphore_wait(barrier, total - 1)

    def along(k):
        return lax.rem(row_me + k, parties)

    def row_copies(which, pick_src, pick_dst):
        return [
            remote(
                pick_src(along(k)),
                pick_dst(row_me),
                row_send.at[which, k],
                row_recv.at[which, k],
                along(k),
                col_me,
            )
            for k in range(1, parties)
        ]

    def edge_copies(which, src, dst):
        return [
            [
                remote(
                    src(side),
                    dst(1 - side),
                    edge_send.at[which, side, k],
                    edge_recv.at[which, side, k],
                    along(k),
                    jnp.maximum(col_me - 1, 0)
                    if side == 0
                    else jnp.minimum(col_me + 1, strips - 1),
                )
                for k in range(parties)
            ]
            for side in range(2)
        ]

    def run_edges(copies, action):
        for side in range(2):
            sends = (col_me > 0) if side == 0 else (col_me < strips - 1)
            takes = (col_me < strips - 1) if side == 0 else (col_me > 0)

            @pl.when(takes if action == "recv" else sends)
            def _():
                for copy in copies[side]:
                    if action == "start":
                        copy.start()
                    elif action == "recv":
                        copy.wait_recv()
                    else:
                        copy.wait_send()

    stat0 = stat_copies(0)
    patch0 = row_copies(0, lambda t: patches.at[row_me], lambda me_row: patches.at[me_row])
    edge0 = edge_copies(0, lambda s: edge_out.at[s], lambda s: edges.at[s, row_me])
    for copy in stat0:
        copy.start()
    for copy in patch0:
        copy.start()
    run_edges(edge0, "start")

    pair_copies = [
        remote(
            stale_ref,
            pairs.at[col_me],
            pair_send.at[k],
            pair_recv.at[k],
            row_me,
            lax.rem(col_me + k, strips),
        )
        for k in range(1, strips)
    ]
    half = block // 2
    halves = (pl.ds(0, half), pl.ds(half, half))
    back = [
        row_copies(
            3 + part,
            lambda t: w_back.at[row_me, halves[part]],
            lambda me_row: w_back.at[me_row, halves[part]],
        )
        for part in range(2)
    ]

    for copy in patch0:
        copy.wait_recv()
    run_edges(edge0, "recv")

    load_back.wait()
    for copy in pair_copies:
        copy.start()
    for copy in back[0]:
        copy.start()

    at, source = iota2((strip_cells, strip_cells), 0), iota2((strip_cells, strip_cells), 1)
    at_col, at_row = lax.div(at, rows_all), lax.rem(at, rows_all)
    to_columns = one_hot(source == at_row * cols + at_col)
    at_row, at_col = lax.div(at, cols), lax.rem(at, cols)
    to_rows = one_hot(source == at_col * rows_all + at_row)

    strip[rows_all : rows_all + strip_cells] = matmul(
        to_columns, patches[...].reshape(strip_cells, width)
    )
    arrived = edges[...].reshape(2 * parties * pad, LANES)
    at = iota2((2 * rows_all, 2 * parties * pad), 0)
    source = iota2((2 * rows_all, 2 * parties * pad), 1)
    for j in range(parts):
        chosen = one_hot(source == lax.div(at, rows) * pad + j * rows + lax.rem(at, rows))
        part = matmul(chosen, arrived)
        span = slice(j * LANES, (j + 1) * LANES)
        strip[:rows_all, span] = part[:rows_all]
        strip[rows_all + strip_cells :, span] = part[rows_all:]

    for copy in stat0:
        copy.wait_recv()

    where_at = iota2((halo_cells, 1), 0)
    outside = ((where_at < rows_all) & (col_me == 0)) | (
        (where_at >= rows_all + strip_cells) & (col_me == strips - 1)
    )
    in_column = lax.rem(where_at, rows_all)

    def activate(which, field):
        normed = norm(which, field)
        act = jnp.where(outside, 0.0, normed / (1.0 + jnp.exp(-normed)))
        acts[1] = act.astype(BF)
        acts[0] = jnp.where(in_column == 0, 0.0, pltpu.roll(act, 1, 0)).astype(BF)
        acts[2] = jnp.where(
            in_column == rows_all - 1, 0.0, pltpu.roll(act, halo_cells - 1, 0)
        ).astype(BF)

    def convolve(which, weights):
        result = jnp.zeros((strip_cells, block), F32)
        for a, b in taps:
            loads[which][3 * a + b].wait()
            result = result + times_rows(
                acts[a, b * rows_all : b * rows_all + strip_cells], weights[3 * a + b]
            )
        return result

    activate(0, strip[...])

    first = convolve(0, w_one)
    offset = bias_ref[0:1] + time_ref[...].reshape(1, width)
    middle = pl.ds(rows_all, strip_cells)
    raw[row_me, rows_all : rows_all + strip_cells] = first.astype(BF)
    raw1 = row_copies(1, lambda t: raw.at[row_me, middle], lambda me_row: raw.at[me_row, middle])
    ends_src = (pl.ds(rows_all, rows_all), pl.ds(strip_cells, rows_all))
    ends_dst = (pl.ds(0, rows_all), pl.ds(rows_all + strip_cells, rows_all))
    edge1 = edge_copies(
        1, lambda s: raw.at[row_me, ends_src[s]], lambda s: raw.at[row_me, ends_dst[s]]
    )
    for copy in raw1:
        copy.start()
    run_edges(edge1, "start")
    send_stats(1, first + mine(offset), block_groups)
    stat1 = stat_copies(1)
    for copy in stat1:
        copy.start()

    @pl.when(col_me == 0)
    def _():
        raw[:, :rows_all] = jnp.zeros((parties, rows_all, block), BF)

    @pl.when(col_me == strips - 1)
    def _():
        raw[:, rows_all + strip_cells :] = jnp.zeros((parties, rows_all, block), BF)

    residual = mine(strip[rows_all : rows_all + strip_cells]) + mine(bias_ref[1:2])

    for copy in raw1:
        copy.wait_recv()
    run_edges(edge1, "recv")
    for copy in back[1]:
        copy.start()
    field = jnp.concatenate([raw[i].astype(F32) for i in range(parties)], axis=1) + offset
    for copy in stat1:
        copy.wait_recv()
    activate(1, field)
    second = convolve(1, w_two)

    rounded = (residual + second).astype(BF)
    res[row_me] = rounded
    res2 = row_copies(2, lambda t: res.at[row_me], lambda me_row: res.at[me_row])
    for copy in res2:
        copy.start()
    send_stats(2, rounded.astype(F32), block_groups)
    stat2 = stat_copies(2)
    for copy in stat2:
        copy.start()
    for copy in res2:
        copy.wait_recv()
    field = jnp.concatenate([res[i].astype(F32) for i in range(parties)], axis=1)
    at, source = iota2((cells, strip_cells), 0), iota2((cells, strip_cells), 1)
    patch_row = row_me * rows + lax.div(at, cols)
    chosen = one_hot(source == lax.rem(at, cols) * rows_all + patch_row)
    kept = matmul(chosen, field.astype(BF))
    load_in.wait()
    for copy in stat2:
        copy.wait_recv()
    attn_in = norm(2, field).astype(BF)

    queries = times_rows(attn_in, w_in[:HEAD]).astype(BF)
    fresh = times_rows(attn_in, w_in[HEAD:]).astype(BF)
    for copy in pair_copies:
        copy.wait_recv()
    pairs[col_me] = fresh
    fresh_ref[...] = matmul(to_rows, fresh).astype(BF)
    both = pairs[...].reshape(strips * strip_cells, 2 * HEAD)
    scores = times_rows(queries, both[:, :HEAD]) * (HEAD**-0.5)
    weights = jnp.exp(scores - jnp.max(scores, axis=1, keepdims=True))
    denominator = jnp.sum(weights, axis=1, keepdims=True)
    attended = (matmul(weights.astype(BF), both) / denominator)[:, HEAD:].astype(BF)
    att_out[...] = (
        matmul(to_rows, attended).astype(BF).reshape(parties, cells, HEAD)
    )
    att3 = row_copies(5, lambda t: att_out.at[t], lambda me_row: att.at[me_row])
    for copy in att3:
        copy.start()
    att[row_me] = att_out[row_me]
    for copy in back[0] + back[1]:
        copy.wait_recv()
    for copy in att3:
        copy.wait_recv()
    heads = jnp.concatenate([att[i].astype(F32) for i in range(parties)], axis=1).astype(BF)
    added = jnp.concatenate([times_rows(heads, w_back[i]) for i in range(parties)], axis=1)
    result = kept + added
    for i in range(rows):
        next_ref[i] = result[i * cols : (i + 1) * cols].astype(BF)

    for copy in stat0 + stat1 + stat2 + patch0 + raw1 + res2 + back[0] + back[1] + att3 + pair_copies:
        copy.wait_send()
    run_edges(edge0, "send")
    run_edges(edge1, "send")


def fused(
    latent,
    norm_scale,
    norm_shift,
    time_shift,
    conv_bias,
    conv_one,
    conv_two,
    w_qkv,
    w_out,
    stale_kv,
):
    rows, cols, width = latent.shape
    block = conv_one.shape[2]
    parties, strips = lax.axis_size("prow"), lax.axis_size("pcol")
    total = parties * strips
    rows_all = rows * parties
    cells = rows * cols
    strip_cells = rows_all * cols
    halo_cells = rows_all * (cols + 2)
    pad = -(-rows * (width // LANES) // 16) * 16
    dims = (parties, strips, rows, cols, width, block)
    vmem = pl.BlockSpec(memory_space=pltpu.VMEM)
    hbm = pl.BlockSpec(memory_space=pltpu.HBM)
    dma = pltpu.SemaphoreType.DMA
    next_latent, fresh = pl.pallas_call(
        functools.partial(fused_kernel, dims),
        out_shape=(
            jax.ShapeDtypeStruct(latent.shape, BF),
            jax.ShapeDtypeStruct((strip_cells, 2 * HEAD), BF),
        ),
        in_specs=[hbm] * 10,
        out_specs=(vmem, vmem),
        scratch_shapes=[
            pltpu.VMEM(latent.shape, BF),
            pltpu.VMEM(norm_scale.shape, F32),
            pltpu.VMEM(norm_shift.shape, F32),
            pltpu.VMEM(time_shift.shape, F32),
            pltpu.VMEM(conv_bias.shape, F32),
            pltpu.VMEM((9, block, width), BF),
            pltpu.VMEM((9, block, width), BF),
            pltpu.VMEM(w_qkv.shape, BF),
            pltpu.VMEM((parties,) + w_out.shape, BF),
            pltpu.VMEM((parties, cells, width), BF),
            pltpu.VMEM((2, pad, LANES), BF),
            pltpu.VMEM((2, parties, pad, LANES), BF),
            pltpu.VMEM((halo_cells, width), F32),
            pltpu.VMEM((3, halo_cells, width), BF),
            pltpu.VMEM((parties, halo_cells, block), BF),
            pltpu.VMEM((parties, strip_cells, block), BF),
            pltpu.VMEM((strips, strip_cells, 2 * HEAD), BF),
            pltpu.VMEM((parties, cells, HEAD), BF),
            pltpu.VMEM((parties, cells, HEAD), BF),
            pltpu.VMEM((3, total, 2, 128), F32),
            pltpu.VMEM((width, 128), BF),
            dma((25,)),
            dma((3, total)),
            dma((3, total)),
            dma((6, parties)),
            dma((6, parties)),
            dma((2, 2, parties)),
            dma((2, 2, parties)),
            dma((strips,)),
            dma((strips,)),
        ],
        compiler_params=pltpu.CompilerParams(
            collective_id=0, has_side_effects=True, vmem_limit_bytes=63 * 2**20
        ),
    )(
        latent,
        norm_scale,
        norm_shift,
        time_shift,
        conv_bias,
        conv_one,
        conv_two,
        w_qkv,
        w_out,
        stale_kv.reshape(strip_cells, 2 * HEAD),
    )
    return next_latent, fresh.reshape(rows_all, cols, 1, 2 * HEAD)


def solution(mesh):
    placed = (
        P("prow", "pcol", None),
        P(),
        P(),
        P(),
        P(),
        P(None, None, "prow", None),
        P(None, None, "prow", None),
        P("prow", None),
        P("prow", None),
        P(None, "pcol", "prow", None),
    )

    def body(*args):
        return (fused if fits(mesh, *args) else shards)(*args)

    return jax.shard_map(
        body,
        mesh=mesh,
        in_specs=placed,
        out_specs=(P("prow", "pcol", None), P(None, "pcol", "prow", None)),
        check_vma=False,
    )
```
